32 devices in a mesh: strike: 8 (over z, x), dip: 4 (over y, core).
Axes of the slice: x: 2, y: 2, z: 4, core: 2. Of those that a mesh axis runs over, the one named last changes fastest.
Arguments:
- pressure: float32 [64, 512, 512], P(None, 'strike', 'dip'), may hold values from -6 to 6
- strike_vel: float32 [64, 512, 512], P(None, 'strike', 'dip'), may hold values from -6 to 6
- dip_vel: float32 [64, 512, 512], P(None, 'strike', 'dip'), may hold values from -6 to 6
- bathy_class: int32 [512, 512], P('strike', 'dip'), may hold values from 0 to 7
- bulk_table: float32 [8], replicated, may hold values from 0.5 to 2
- buoy_table: float32 [8], replicated, may hold values from 0.5 to 2
- gravity: float32 [64], replicated, may hold values from 0.5 to 2
- sensor_amp: float32 [4, 256], P(None, ('strike', 'dip')), may hold values from -12 to 12
- sensor_owner: int32 [256, 1], P(('strike', 'dip')), may hold values from 0 to 3; in each aligned block of 8 rows (0 to 7, 8 to 15, ...) at most 2 rows name the same one
- sensor_cell: int32 [256], P(('strike', 'dip')), may hold values from 0 to 8191
- probe_kernel: bfloat16 [96, 512, 512], P(None, 'strike', 'dip'), may hold values from -6 to 6
Outputs:
- final_pressure: float32 [64, 512, 512], P(None, 'strike', 'dip')
- panel_factor: float32 [96, 96], replicated
The draws below stay inside these ranges and needn't reach their ends.
Inputs may be any that keep to these rules, and one draw needn't show every extreme that they name: `sensor_owner`: the owner lies in the same strike index as the device that holds the sensor; among the 8 sensors of one device at most 2 name the same owner, a bound that some block reaches. `sensor_cell`: numbered row by row within the owner's block, 128 cells a row.
All inputs are finite; a program needn't handle non-finite values.
Results may differ from the reference program's by a relative error of at most 0.0003.
Values sent between devices are 32-bit elements; how exact they have to be, the bound alone decides.
A program may use at most 128 MiB of HBM per device.

```python
import math
import jax
import jax.numpy as jnp
import numpy as np
from jax import lax

CX = 64
CY = 128
LEV = 64
STEPS = 4
PROBES = 96
NCLASS = 8
S_DEV = 8
CAP = 2
NX = 512
NY = 512
SENSORS = 256
N_STRIKE = 8
N_DIP = 4


def with_ends(entries, own_key, smallest, high):
    extent = entries.shape
    spot = [jax.random.randint(jax.random.fold_in(own_key, axis), (), 0, extent[axis]) for axis in range(len(extent))]
    entries = entries.at[tuple(spot)].set(smallest)
    longest = extent.index(max(extent))
    spot[longest] = (spot[longest] + 1) % extent[longest]
    return entries.at[tuple(spot)].set(high)


def level_of(key, dims, cuts, least, top_value):
    def one(axis_at, parts):
        steps = jax.random.uniform(jax.random.fold_in(jax.random.fold_in(key, 6), axis_at), (parts,), jnp.float32, least / len(cuts), top_value / len(cuts))
        return jnp.repeat(jnp.exp(steps), dims[axis_at] // parts).reshape((-1,) + (1,) * (len(dims) - axis_at - 1))

    factor_of = one(*cuts[0])
    for cut in cuts[1:]:
        factor_of = factor_of * one(*cut)
    return factor_of


def routed_block(stream_key, own, number, rows, amount, top, reach, slope):
    sequence = jax.random.permutation(stream_key, amount)
    packed, ordinary = shares(amount, rows * top, reach, slope, True), shares(amount, rows * top, reach, slope, False)
    places = jnp.arange(amount)

    def named(lengths, rotation):
        used = int((lengths > 0).sum())
        fixed = max(1, used // 4)
        passed = fixed + (places - fixed + rotation * (used - fixed)) % max(1, amount - fixed)
        return jnp.zeros((amount,), jnp.int32).at[sequence[jnp.where(places < fixed, places, passed)]].set(jnp.asarray(lengths, jnp.int32))

    lengths = jnp.where(number % 4 == 0, named(packed, number // 4), named(ordinary, number - number // 4 - 1))
    mixed = jax.random.permutation(jax.random.fold_in(own, 3), amount)
    giver, sink = mixed[0:amount // 2 * 2:2], mixed[1:amount // 2 * 2:2]
    room = jnp.minimum(lengths[giver] - 1, reach - lengths[sink]) // 2
    room = jnp.where((giver == sequence[0]) | (sink == sequence[0]) | (lengths[sink] == 0), 0, jnp.maximum(room, 0))
    passed = jax.random.randint(jax.random.fold_in(own, 4), (amount // 2,), 0, 1 << 20) % (room + 1)
    lengths = lengths.at[giver].add(-passed).at[sink].add(passed)
    items = jnp.searchsorted(jnp.cumsum(lengths), jnp.arange(rows * top), side="right").astype(jnp.int32)
    grid = items.reshape(top, rows).T
    grid = grid[jax.random.permutation(jax.random.fold_in(own, 1), rows)]
    rotation = jax.random.randint(jax.random.fold_in(own, 2), (rows, 1), 0, top)
    return jnp.take_along_axis(grid, (jnp.arange(top)[None, :] + rotation) % top, axis=1)


def shares(count, total, limit, skew, full):
    loads = [(1 << 20) // math.isqrt(standing ** skew) + 1 for standing in range(1, count + 1)]
    largest = limit if full else min(limit, max(-(-total // count), total * loads[0] // sum(loads)))
    least = 1 if total - largest >= count - 1 else 0
    holding, surplus = [largest] + [least] * (count - 1), total - largest - least * (count - 1)
    while surplus > 0:
        free = [i for i in range(1, count) if holding[i] < largest] or [i for i in range(1, count) if holding[i] < limit]
        pool, remaining = sum([loads[i] for i in free]), surplus
        for i in free:
            addition = min(limit - holding[i], max(1, remaining * loads[i] // pool), surplus)
            holding[i] = holding[i] + addition
            surplus = surplus - addition
    return np.array(holding)


def normal_values(own_key, extent, scale, bound, cuts=(), held_as=jnp.bfloat16):
    loudness = level_of(own_key, extent, cuts, -0.22, 0.18) if cuts else 1.0
    values = jax.random.normal(own_key, extent, jnp.float32) * scale * loudness
    return jnp.minimum(jnp.maximum(values, -bound), bound).astype(held_as)


def setup_inputs(seed: int = 0) -> dict:
    keys = jax.random.split(jax.random.key(seed), 12)
    pressure = normal_values(keys[0], (LEV, NX, NY), 1.0, 6.0, ((1, 8), (2, 4)), jnp.float32)
    strike_vel = normal_values(keys[1], (LEV, NX, NY), 1.0, 6.0, ((1, 8), (2, 4)), jnp.float32)
    dip_vel = normal_values(keys[2], (LEV, NX, NY), 1.0, 6.0, ((1, 8), (2, 4)), jnp.float32)
    bathy_class = with_ends(jax.random.randint(keys[3], (NX, NY), 0, NCLASS), jax.random.fold_in(keys[3], 1), 0, NCLASS - 1).astype(jnp.int32)
    bulk_table = jnp.clip(jnp.exp(jax.random.uniform(keys[4], (NCLASS,), jnp.float32, math.log(0.5), math.log(2.0))), 0.5, 2.0)
    buoy_table = jnp.clip(jnp.exp(jax.random.uniform(keys[5], (NCLASS,), jnp.float32, math.log(0.5), math.log(2.0))), 0.5, 2.0)
    gravity = jnp.clip(jnp.exp(jax.random.uniform(keys[6], (LEV,), jnp.float32, math.log(0.5), math.log(2.0))), 0.5, 2.0)
    sensor_amp = normal_values(keys[7], (STEPS, SENSORS), 2.0, 12.0, ((1, 32),), jnp.float32)
    sensor_owner_keys = jax.random.split(jax.random.fold_in(keys[8], 1), SENSORS // S_DEV)
    sensor_owner_turns = jax.random.permutation(jax.random.fold_in(keys[8], 3), SENSORS // S_DEV)
    sensor_owner = jax.vmap(lambda own, number: routed_block(jax.random.fold_in(keys[8], 2), own, number, S_DEV, N_DIP, 1, CAP, 2))(sensor_owner_keys, sensor_owner_turns).reshape((SENSORS, 1))
    sensor_cell = with_ends(jax.random.randint(keys[9], (SENSORS,), 0, CX * CY), jax.random.fold_in(keys[9], 1), 0, (CX * CY) - 1).astype(jnp.int32)
    probe_kernel = normal_values(keys[10], (PROBES, NX, NY), 1.0, 6.0, ((1, 8), (2, 4)))
    return {"pressure": pressure, "strike_vel": strike_vel, "dip_vel": dip_vel, "bathy_class": bathy_class, "bulk_table": bulk_table, "buoy_table": buoy_table, "gravity": gravity, "sensor_amp": sensor_amp, "sensor_owner": sensor_owner, "sensor_cell": sensor_cell, "probe_kernel": probe_kernel}


time_step = 0.2

def fourth_diff(extended, axis):
    length = extended.shape[axis] - 4

    def window(offset):
        return lax.slice_in_dim(extended, offset, offset + length, axis=axis)
    return (8.0 * (window(3) - window(1)) - (window(4) - window(0))) / 12.0

def pad_axis(field, axis, width):
    widths = [(0, 0)] * field.ndim
    widths[axis] = (width, width)
    return jnp.pad(field, widths)

def depth_diff(field):
    padded = pad_axis(field, 0, 1)
    return (padded[2:] - padded[:-2]) / 2.0

def grow_both(field):
    return pad_axis(pad_axis(field, 1, 2), 2, 2)

def grow_strike(field):
    return pad_axis(field, 1, 2)

def grow_dip(field):
    return pad_axis(field, 2, 2)

def lookup(classes, table):
    labels = jnp.arange(NCLASS, dtype=jnp.int32)[:, None, None]
    return lax.optimization_barrier(jnp.sum(jnp.where(classes[None] == labels, table[:, None, None], 0.0), axis=0))

def reference(pressure, strike_vel, dip_vel, bathy_class, bulk_table, buoy_table, gravity, sensor_amp, sensor_owner, sensor_cell, probe_kernel):
    bulk = lookup(bathy_class, bulk_table)
    buoy = lookup(bathy_class, buoy_table)
    sensor_index = jnp.arange(SENSORS, dtype=jnp.int32)
    strike_of = sensor_index // (S_DEV * N_DIP)
    row_index = strike_of * CX + sensor_cell // CY
    column_index = sensor_owner[:, 0] * CY + sensor_cell % CY
    inject = jnp.zeros((STEPS, NX, NY), pressure.dtype).at[:, row_index, column_index].add(sensor_amp)
    vertical = jnp.zeros_like(pressure)
    for step in range(STEPS):
        extended = grow_both(pressure)
        strike_vel = strike_vel - time_step * buoy * fourth_diff(extended[:, :, 2:-2], 1)
        dip_vel = dip_vel - time_step * buoy * fourth_diff(extended[:, 2:-2, :], 2)
        vertical = vertical - time_step * buoy * depth_diff(pressure)
        divergence = fourth_diff(grow_strike(strike_vel), 1) + fourth_diff(grow_dip(dip_vel), 2) + depth_diff(vertical)
        pressure = pressure - time_step * bulk * divergence + time_step * gravity[:, None, None] * vertical
        pressure = pressure.at[-1].add(inject[step])
    seafloor = pressure[-1]
    scale = 1.0 / math.sqrt(NX * NY)

    def accumulate(block, total):
        start = (block * CX).astype(jnp.int32)
        rows_now = lax.dynamic_slice_in_dim(seafloor, start, CX, 0)
        kernel_now = lax.dynamic_slice_in_dim(probe_kernel, start, CX, 1).astype(pressure.dtype)
        panel = (kernel_now * rows_now[None] * scale).reshape(PROBES, CX * NY)
        return total + jnp.dot(panel, panel.T, precision=lax.Precision.HIGHEST)
    gram = lax.fori_loop(jnp.int32(0), jnp.int32(N_STRIKE), accumulate, jnp.zeros((PROBES, PROBES), pressure.dtype))
    panel_factor = jnp.linalg.cholesky(gram).T
    return (pressure, panel_factor)
```

```python
import functools
import math

import jax
import jax.numpy as jnp
from jax import lax
from jax.experimental import pallas as pl
from jax.experimental.pallas import tpu as pltpu
from jax.sharding import PartitionSpec as P

MESH = pl.DeviceIdType.MESH
STEPS = 4
NCLASS = 8
TIME_STEP = 0.2
OFF = 16
CH = 16


def lane_diff(f):
    n = f.shape[-1]
    ax = f.ndim - 1
    near = pltpu.roll(f, n - 1, ax) - pltpu.roll(f, 1, ax)
    far = pltpu.roll(f, n - 2, ax) - pltpu.roll(f, 2, ax)
    return 8.0 * near - far


def kernel(
    ns,
    nd,
    scale,
    bulk_t,
    buoy_t,
    grav,
    classes,
    sens,
    p_hbm,
    sv_hbm,
    dv_hbm,
    k_hbm,
    out_p,
    out_g,
    pe,
    se,
    dv,
    vv,
    kv,
    kf,
    kt,
    bx,
    bk,
    bq,
    hb,
    inj,
    wrow,
    sp_lo,
    sp_hi,
    rp_lo,
    rp_hi,
    sq,
    rq_l,
    rq_r,
    ss_lo,
    ss_hi,
    rs_lo,
    rs_hi,
    sdq,
    rd_l,
    rd_r,
    rb_lo,
    rb_hi,
    rbq_l,
    rbq_r,
    hv,
    qv,
    edge_a,
    edge_b,
    sens_all,
    gram,
    part1,
    part2,
    in_sem,
    out_sem,
    halo_s,
    halo_r,
    vel_s,
    vel_r,
    buo_s,
    buo_r,
    sens_s,
    sens_r,
    red1_s,
    red1_r,
    red2_s,
    red2_r,
    red3_s,
    red3_r,
):
    levels = p_hbm.shape[0]
    rows = p_hbm.shape[1]
    nch = levels // CH
    probes = k_hbm.shape[0]
    si = lax.axis_index("strike")
    di = lax.axis_index("dip")
    END = OFF + rows

    def strike_peer(o):
        return (lax.rem(si + o, ns), di)

    def dip_peer(o):
        return (si, lax.rem(di + o, nd))

    has = (si > 0, si < ns - 1, di > 0, di < nd - 1)
    peer = ((si - 1, di), (si + 1, di), (si, di - 1), (si, di + 1))

    in_p = pltpu.make_async_copy(p_hbm, pe.at[pl.ds(1, levels), pl.ds(OFF, rows), :], in_sem.at[0])
    in_s = pltpu.make_async_copy(sv_hbm, se.at[:, pl.ds(OFF, rows), :], in_sem.at[1])
    in_d = pltpu.make_async_copy(dv_hbm, dv, in_sem.at[2])
    in_k = pltpu.make_async_copy(k_hbm, kv, in_sem.at[3])
    in_p.start()
    in_s.start()
    in_d.start()
    in_k.start()

    barrier = pltpu.get_barrier_semaphore()
    for o in range(1, ns):
        pl.semaphore_signal(barrier, inc=1, device_id=strike_peer(o), device_id_type=MESH)
    for o in range(1, nd):
        pl.semaphore_signal(barrier, inc=1, device_id=dip_peer(o), device_id_type=MESH)

    lane = lax.broadcasted_iota(jnp.int32, (rows, 128), 1)
    slot = lane // 8
    low = (lane % 8) < 4
    rim = (lane < 2) | (lane >= 126)

    cls = classes[...]
    buoy = jnp.zeros((rows, 128), jnp.float32)
    bulk = jnp.zeros((rows, 128), jnp.float32)
    for i in range(NCLASS):
        buoy = jnp.where(cls == i, buoy_t[i], buoy)
        bulk = jnp.where(cls == i, bulk_t[i], bulk)
    bk[...] = bulk * (TIME_STEP / 12.0)
    bx[pl.ds(OFF, rows), :] = buoy * (TIME_STEP / 12.0)
    first = jnp.where(lane < 8, pltpu.roll(buoy * (TIME_STEP / 12.0), 4, 1), 0.0)
    for width in (8, 16, 32, 64):
        first = first + pltpu.roll(first, width, 1)
    bq[...] = first

    zero_block = jnp.zeros((rows, 128), jnp.float32)
    pe[0, pl.ds(OFF, rows), :] = zero_block
    pe[levels + 1, pl.ds(OFF, rows), :] = zero_block
    vv[0] = zero_block
    vv[levels + 1] = zero_block

    def zero_when(cond, *refs):
        @pl.when(jnp.logical_not(cond))
        def _():
            for r in refs:
                r[...] = jnp.zeros(r.shape, r.dtype)

    zero_when(has[0], rp_lo, rs_lo, rb_lo)
    zero_when(has[1], rp_hi, rs_hi, rb_hi)
    zero_when(has[2], rq_l, rd_l, rbq_l)
    zero_when(has[3], rq_r, rd_r, rbq_r)

    pl.semaphore_wait(barrier, ns - 1 + nd - 1)

    def remote(src, dst, s, r, to):
        return pltpu.make_async_remote_copy(
            src_ref=src, dst_ref=dst, send_sem=s, recv_sem=r, device_id=to, device_id_type=MESH
        )

    def halo_copy(k, c, i):
        src = (sp_lo, sp_hi, sq, sq)[i].at[k, c]
        dst = (rp_hi, rp_lo, rq_r, rq_l)[i].at[k, c]
        return remote(src, dst, halo_s.at[k, c, i], halo_r.at[k, c, i], peer[i])

    def vel_copy(c, i):
        src = (ss_lo, ss_hi, sdq, sdq)[i].at[c]
        dst = (rs_hi, rs_lo, rd_r, rd_l)[i].at[c]
        return remote(src, dst, vel_s.at[c, i], vel_r.at[c, i], peer[i])

    def buo_copy(i):
        src = (bx.at[pl.ds(OFF, 8), :], bx.at[pl.ds(END - 8, 8), :], bq, bq)[i]
        dst = (rb_hi, rb_lo, rbq_r, rbq_l)[i]
        return remote(src, dst, buo_s.at[i], buo_r.at[i], peer[i])

    def each_side(make, what):
        for i in range(4):
            cond = has[i ^ 1] if what == "recv" else has[i]

            @pl.when(cond)
            def _(i=i):
                copy = make(i)
                if what == "start":
                    copy.start()
                elif what == "recv":
                    copy.wait_recv()
                else:
                    copy.wait_send()

    def sens_copy(o):
        return remote(sens, sens_all.at[di], sens_s.at[o - 1], sens_r.at[o - 1], dip_peer(o))

    each_side(buo_copy, "start")
    for o in range(1, nd):
        sens_copy(o).start()

    zero_pack = jnp.zeros((rows, 128), jnp.float32)

    def packed(acc, field, j):
        return jnp.where(slot == j, pltpu.roll(field, 8 * j + 4, 1), acc)

    in_p.wait()
    in_s.wait()
    in_d.wait()

    for c in reversed(range(nch)):

        def pack_first(j, accs, c=c):
            lev = c * CH + j
            f = pe[lev + 1, pl.ds(OFF, rows), :]
            sp_lo[0, c, j] = f[0:4]
            sp_hi[0, c, j] = f[rows - 4 : rows]
            ss_lo[c, j] = se[lev, pl.ds(OFF, 8), :][0:2]
            ss_hi[c, j] = se[lev, pl.ds(END - 8, 8), :][6:8]
            return packed(accs[0], f, j), packed(accs[1], dv[lev], j)

        a, b = lax.fori_loop(0, CH, pack_first, (zero_pack, zero_pack))
        sq[0, c] = a
        sdq[c] = b
        each_side(lambda i, c=c: halo_copy(0, c, i), "start")
        each_side(lambda i, c=c: vel_copy(c, i), "start")

    in_k.wait()

    def widen(i, _):
        kf[pl.ds(pl.multiple_of(i * rows, rows), rows), :] = kv[i].astype(jnp.float32)
        return 0

    lax.fori_loop(0, probes, widen, 0)
    half = rows // 2

    def regroup(x, _):
        kt[x, :, 0:128] = kf[pl.ds(x, probes, stride=rows), :].astype(jnp.bfloat16)
        kt[x, :, 128:256] = kf[pl.ds(x + half, probes, stride=rows), :].astype(jnp.bfloat16)
        return 0

    lax.fori_loop(0, half, regroup, 0)

    sens_all[di] = sens[...]
    for o in range(1, nd):
        sens_copy(o).wait_recv()
    every = sens_all[...].reshape(nd * 8, 128)
    mine = every[:, 5:6] == di.astype(jnp.float32)
    cell = every[:, 4:5].astype(jnp.int32)
    slane = lax.broadcasted_iota(jnp.int32, (nd * 8, 128), 1)
    at_row = (lax.shift_right_logical(cell, 7) == slane) & mine
    at_col = ((cell & 127) == slane).astype(jnp.float32)
    for k in range(STEPS):
        left = jnp.where(at_row, every[:, k : k + 1], 0.0)
        placed = lax.dot_general(
            left,
            at_col,
            (((0,), (0,)), ((), ())),
            precision=lax.Precision.HIGHEST,
            preferred_element_type=jnp.float32,
        )
        inj[k] = placed[0:rows]

    each_side(buo_copy, "recv")
    bx[pl.ds(OFF - 8, 8), :] = rb_lo[...]
    bx[pl.ds(END, 8), :] = rb_hi[...]
    hb[...] = jnp.where(low, rbq_l[...], rbq_r[...])

    def phase_a(k, c):
        each_side(lambda i: halo_copy(k, c, i), "recv")
        if k == 0:
            each_side(lambda i: vel_copy(c, i), "recv")
            hv[c] = jnp.where(low, rd_l[c], rd_r[c])
        own = sq[k, c]
        d_left = lane_diff(jnp.where(low, rq_l[k, c], own))
        d_right = lane_diff(jnp.where(low, own, rq_r[k, c]))
        hv[c] = hv[c] - hb[...] * jnp.where(low, d_left, d_right)
        edge_a[...] = jnp.where(low, d_right, d_left)

        def level(j, acc):
            lev = c * CH + j
            pe[lev + 1, pl.ds(OFF - 4, 4), :] = rp_lo[k, c, j]
            pe[lev + 1, pl.ds(END, 4), :] = rp_hi[k, c, j]
            if k == 0:
                se[lev, pl.ds(OFF - 2, 2), :] = rs_lo[c, j]
                se[lev, pl.ds(END, 2), :] = rs_hi[c, j]

            def win(o):
                return pe[lev + 1, pl.ds(OFF - 8 + o, rows + 16), :]

            ds = 8.0 * (win(1) - win(-1)) - (win(2) - win(-2))
            ext = pl.ds(OFF - 8, rows + 16)
            se[lev, ext, :] = se[lev, ext, :] - bx[ext, :] * ds
            own_rows = pl.ds(OFF, rows)
            b = bx[own_rows, :]
            dd = jnp.where(rim, pltpu.roll(edge_a[...], 124 - 8 * j, 1), lane_diff(pe[lev + 1, own_rows, :]))
            v = dv[lev] - b * dd
            dv[lev] = v
            dz = (6.0 * b) * (pe[lev + 2, own_rows, :] - pe[lev, own_rows, :])
            vv[lev + 1] = -dz if k == 0 else vv[lev + 1] - dz
            return packed(acc, v, j)

        qv[c] = lax.fori_loop(0, CH, level, zero_pack)

    def phase_b(k, c):
        last = k == STEPS - 1
        own = qv[c]
        halo = hv[c]
        d_left = lane_diff(jnp.where(low, halo, own))
        d_right = lane_diff(jnp.where(low, own, halo))
        edge_b[...] = jnp.where(low, d_right, d_left)

        def level(j, acc):
            lev = c * CH + j

            def win(o):
                return se[lev, pl.ds(OFF + o, rows), :]

            ds = 8.0 * (win(1) - win(-1)) - (win(2) - win(-2))
            dd = jnp.where(rim, pltpu.roll(edge_b[...], 124 - 8 * j, 1), lane_diff(dv[lev]))
            dz = 6.0 * (vv[lev + 2] - vv[lev])
            own_rows = pl.ds(OFF, rows)
            f = pe[lev + 1, own_rows, :] - bk[...] * (ds + dd + dz) + (TIME_STEP * grav[lev]) * vv[lev + 1]
            if c == nch - 1:
                f = f + jnp.where(j == CH - 1, inj[k], 0.0)
            pe[lev + 1, own_rows, :] = f
            if last:
                return acc
            sp_lo[k + 1, c, j] = f[0:4]
            sp_hi[k + 1, c, j] = f[rows - 4 : rows]
            return packed(acc, f, j)

        acc = lax.fori_loop(0, CH, level, zero_pack)
        if not last:
            sq[k + 1, c] = acc
            each_side(lambda i: halo_copy(k + 1, c, i), "start")
        else:
            out_copy(c).start()

    def out_copy(c):
        return pltpu.make_async_copy(
            pe.at[pl.ds(1 + c * CH, CH), pl.ds(OFF, rows), :], out_p.at[pl.ds(c * CH, CH)], out_sem.at[c]
        )

    share = gram.shape[1]

    def red1(o):
        to = lax.rem(di + o, nd)
        return remote(gram.at[to], part1.at[o - 1], red1_s.at[o - 1], red1_r.at[o - 1], dip_peer(o))

    def red2(o):
        return remote(part2.at[si], part2.at[si], red2_s.at[o - 1], red2_r.at[o - 1], strike_peer(o))

    def red3(o):
        return remote(out_g.at[di], out_g.at[di], red3_s.at[o - 1], red3_r.at[o - 1], dip_peer(o))

    def reduce_start():
        sea = pe[levels, pl.ds(OFF, rows), :] * scale
        wrow[...] = sea * sea

        def body(x, acc):
            kx = kt[x]
            w = jnp.concatenate([wrow[pl.ds(x, 1), :], wrow[pl.ds(x + half, 1), :]], axis=1)
            kw = kx.astype(jnp.float32) * w
            hi = kw.astype(jnp.bfloat16)
            lo = (kw - hi.astype(jnp.float32)).astype(jnp.bfloat16)
            both = jnp.concatenate([hi, lo], axis=0)
            return acc + lax.dot_general(
                both, kx, (((1,), (1,)), ((), ())), preferred_element_type=jnp.float32
            )

        acc = lax.fori_loop(0, half, body, jnp.zeros((2 * probes, probes), jnp.float32))
        total = acc[0:probes] + acc[probes : 2 * probes]
        total = jnp.concatenate([total, jnp.zeros((probes, 128 - probes), jnp.float32)], axis=1)
        if nd * share > probes:
            total = jnp.concatenate([total, jnp.zeros((nd * share - probes, 128), jnp.float32)], axis=0)
        for d in range(nd):
            gram[d] = total[d * share : (d + 1) * share]
        for o in range(1, nd):
            red1(o).start()

    def reduce_middle():
        s = gram[di]
        for o in range(1, nd):
            red1(o).wait_recv()
            s = s + part1[o - 1]
        part2[si] = s
        for o in range(1, ns):
            red2(o).start()

    def reduce_spread():
        for o in range(1, ns):
            red2(o).wait_recv()
        s = part2[0]
        for i in range(1, ns):
            s = s + part2[i]
        out_g[di] = s
        for o in range(1, nd):
            red3(o).start()

    stages = [reduce_start, reduce_middle, reduce_spread]
    for k in range(STEPS):
        phase_a(k, nch - 1)
        for c in reversed(range(nch)):
            if c > 0:
                phase_a(k, c - 1)
            phase_b(k, c)
            if k == STEPS - 1 and stages:
                stages.pop(0)()
    for stage in stages:
        stage()

    for c in range(nch):
        out_copy(c).wait()
        each_side(lambda i, c=c: vel_copy(c, i), "send")
        for k in range(STEPS):
            each_side(lambda i, c=c, k=k: halo_copy(k, c, i), "send")
    each_side(buo_copy, "send")
    for o in range(1, nd):
        sens_copy(o).wait_send()
        red1(o).wait_send()
        red3(o).wait_recv()
        red3(o).wait_send()
    for o in range(1, ns):
        red2(o).wait_send()


def body(
    ns,
    nd,
    pressure,
    strike_vel,
    dip_vel,
    bathy_class,
    bulk_table,
    buoy_table,
    gravity,
    sensor_amp,
    sensor_owner,
    sensor_cell,
    probe_kernel,
):
    levels, rows, cols = pressure.shape
    probes = probe_kernel.shape[0]
    nch = levels // CH
    share = -(-probes // (8 * nd)) * 8
    scale = 1.0 / math.sqrt(rows * cols * ns * nd)
    sens = jnp.concatenate(
        [
            sensor_amp.T,
            sensor_cell.astype(jnp.float32)[:, None],
            sensor_owner.astype(jnp.float32),
            jnp.zeros((sensor_amp.shape[1], 128 - STEPS - 2), jnp.float32),
        ],
        axis=1,
    )
    f32 = jnp.float32

    def vmem(*shape, dtype=f32):
        return pltpu.VMEM(shape, dtype)

    def sems(*shape):
        return pltpu.SemaphoreType.DMA(shape)

    scratch = [
        vmem(levels + 2, rows + 2 * OFF, cols),
        vmem(levels, rows + 2 * OFF, cols),
        vmem(levels, rows, cols),
        vmem(levels + 2, rows, cols),
        vmem(probes, rows, cols, dtype=jnp.bfloat16),
        vmem(probes * rows, cols),
        vmem(rows // 2, probes, 2 * cols, dtype=jnp.bfloat16),
        vmem(rows + 2 * OFF, cols),
        vmem(rows, cols),
        vmem(rows, cols),
        vmem(rows, cols),
        vmem(STEPS, rows, cols),
        vmem(rows, cols),
        vmem(STEPS, nch, CH, 4, cols),
        vmem(STEPS, nch, CH, 4, cols),
        vmem(STEPS, nch, CH, 4, cols),
        vmem(STEPS, nch, CH, 4, cols),
        vmem(STEPS, nch, rows, cols),
        vmem(STEPS, nch, rows, cols),
        vmem(STEPS, nch, rows, cols),
        vmem(nch, CH, 2, cols),
        vmem(nch, CH, 2, cols),
        vmem(nch, CH, 2, cols),
        vmem(nch, CH, 2, cols),
        vmem(nch, rows, cols),
        vmem(nch, rows, cols),
        vmem(nch, rows, cols),
        vmem(8, cols),
        vmem(8, cols),
        vmem(rows, cols),
        vmem(rows, cols),
        vmem(nch, rows, cols),
        vmem(nch, rows, cols),
        vmem(rows, cols),
        vmem(rows, cols),
        vmem(nd, 8, cols),
        vmem(nd, share, cols),
        vmem(nd - 1, share, cols),
        vmem(ns, share, cols),
        sems(4),
        sems(nch),
        sems(STEPS, nch, 4),
        sems(STEPS, nch, 4),
        sems(nch, 4),
        sems(nch, 4),
        sems(4),
        sems(4),
        sems(nd - 1),
        sems(nd - 1),
        sems(nd - 1),
        sems(nd - 1),
        sems(ns - 1),
        sems(ns - 1),
        sems(nd - 1),
        sems(nd - 1),
    ]
    smem = pl.BlockSpec(memory_space=pltpu.SMEM)
    whole = pl.BlockSpec(memory_space=pltpu.VMEM)
    hbm = pl.BlockSpec(memory_space=pl.ANY)
    final, gram = pl.pallas_call(
        functools.partial(kernel, ns, nd, scale),
        out_shape=(
            jax.ShapeDtypeStruct(pressure.shape, f32),
            jax.ShapeDtypeStruct((nd, share, cols), f32),
        ),
        in_specs=[smem, smem, smem, whole, whole, hbm, hbm, hbm, hbm],
        out_specs=(hbm, whole),
        scratch_shapes=scratch,
        compiler_params=pltpu.CompilerParams(
            collective_id=0, has_side_effects=True, vmem_limit_bytes=48 * 2**20
        ),
    )(bulk_table, buoy_table, gravity, bathy_class, sens, pressure, strike_vel, dip_vel, probe_kernel)
    gram = gram.reshape(nd * share, cols)[:probes, :probes]
    return final, jnp.linalg.cholesky(gram).T


def solution(mesh):
    return jax.shard_map(
        functools.partial(body, mesh.shape["strike"], mesh.shape["dip"]),
        mesh=mesh,
        in_specs=(
            P(None, "strike", "dip"),
            P(None, "strike", "dip"),
            P(None, "strike", "dip"),
            P("strike", "dip"),
            P(),
            P(),
            P(),
            P(None, ("strike", "dip")),
            P(("strike", "dip"), None),
            P(("strike", "dip")),
            P(None, "strike", "dip"),
        ),
        out_specs=(P(None, "strike", "dip"), P()),
        check_vma=False,
    )
```

```python
import functools
import math

import jax
import jax.numpy as jnp
from jax import lax
from jax.experimental import pallas as pl
from jax.experimental.pallas import tpu as pltpu
from jax.sharding import PartitionSpec as P

MESH = pl.DeviceIdType.MESH
STEPS = 4
NCLASS = 8
TIME_STEP = 0.2
OFF = 16
CH = 16


def lane_diff(f):
    n = f.shape[-1]
    ax = f.ndim - 1
    near = pltpu.roll(f, n - 1, ax) - pltpu.roll(f, 1, ax)
    far = pltpu.roll(f, n - 2, ax) - pltpu.roll(f, 2, ax)
    return 8.0 * near - far


def kernel(
    ns,
    nd,
    scale,
    bulk_t,
    buoy_t,
    grav,
    classes,
    sens,
    p_hbm,
    sv_hbm,
    dv_hbm,
    k_hbm,
    out_p,
    out_g,
    pe,
    se,
    dv,
    vv,
    kv,
    kf,
    kt,
    bx,
    bk,
    bq,
    hb,
    inj,
    wrow,
    sp_lo,
    sp_hi,
    rp_lo,
    rp_hi,
    sq,
    rq_l,
    rq_r,
    ss_lo,
    ss_hi,
    rs_lo,
    rs_hi,
    sdq,
    rd_l,
    rd_r,
    rb_lo,
    rb_hi,
    rbq_l,
    rbq_r,
    hv,
    qv,
    edge_a,
    edge_b,
    sens_all,
    gram,
    part1,
    part2,
    in_sem,
    out_sem,
    halo_s,
    halo_r,
    vel_s,
    vel_r,
    buo_s,
    buo_r,
    sens_s,
    sens_r,
    red1_s,
    red1_r,
    red2_s,
    red2_r,
    red3_s,
    red3_r,
):
    levels = p_hbm.shape[0]
    rows = p_hbm.shape[1]
    nch = levels // CH
    probes = k_hbm.shape[0]
    si = lax.axis_index("strike")
    di = lax.axis_index("dip")
    END = OFF + rows

    def strike_peer(o):
        return (lax.rem(si + o, ns), di)

    def dip_peer(o):
        return (si, lax.rem(di + o, nd))

    has = (si > 0, si < ns - 1, di > 0, di < nd - 1)
    peer = ((si - 1, di), (si + 1, di), (si, di - 1), (si, di + 1))

    in_p = pltpu.make_async_copy(p_hbm, pe.at[pl.ds(1, levels), pl.ds(OFF, rows), :], in_sem.at[0])
    in_s = pltpu.make_async_copy(sv_hbm, se.at[:, pl.ds(OFF, rows), :], in_sem.at[1])
    in_d = pltpu.make_async_copy(dv_hbm, dv, in_sem.at[2])
    in_k = pltpu.make_async_copy(k_hbm, kv, in_sem.at[3])
    in_p.start()
    in_s.start()
    in_d.start()
    in_k.start()

    barrier = pltpu.get_barrier_semaphore()
    for o in range(1, ns):
        pl.semaphore_signal(barrier, inc=1, device_id=strike_peer(o), device_id_type=MESH)
    for o in range(1, nd):
        pl.semaphore_signal(barrier, inc=1, device_id=dip_peer(o), device_id_type=MESH)

    lane = lax.broadcasted_iota(jnp.int32, (rows, 128), 1)
    slot = lane // 8
    low = (lane % 8) < 4
    rim = (lane < 2) | (lane >= 126)

    cls = classes[...]
    buoy = jnp.zeros((rows, 128), jnp.float32)
    bulk = jnp.zeros((rows, 128), jnp.float32)
    for i in range(NCLASS):
        buoy = jnp.where(cls == i, buoy_t[i], buoy)
        bulk = jnp.where(cls == i, bulk_t[i], bulk)
    bk[...] = bulk * (TIME_STEP / 12.0)
    bx[pl.ds(OFF, rows), :] = buoy * (TIME_STEP / 12.0)
    first = jnp.where(lane < 8, pltpu.roll(buoy * (TIME_STEP / 12.0), 4, 1), 0.0)
    for width in (8, 16, 32, 64):
        first = first + pltpu.roll(first, width, 1)
    bq[...] = first

    zero_block = jnp.zeros((rows, 128), jnp.float32)
    pe[0, pl.ds(OFF, rows), :] = zero_block
    pe[levels + 1, pl.ds(OFF, rows), :] = zero_block

    def clear(i, _):
        vv[i] = zero_block
        return 0

    lax.fori_loop(0, levels + 2, clear, 0)

    def zero_when(cond, *refs):
        @pl.when(jnp.logical_not(cond))
        def _():
            for r in refs:
                r[...] = jnp.zeros(r.shape, r.dtype)

    zero_when(has[0], rp_lo, rs_lo, rb_lo)
    zero_when(has[1], rp_hi, rs_hi, rb_hi)
    zero_when(has[2], rq_l, rd_l, rbq_l)
    zero_when(has[3], rq_r, rd_r, rbq_r)

    pl.semaphore_wait(barrier, ns - 1 + nd - 1)

    def remote(src, dst, s, r, to):
        return pltpu.make_async_remote_copy(
            src_ref=src, dst_ref=dst, send_sem=s, recv_sem=r, device_id=to, device_id_type=MESH
        )

    def halo_copy(k, c, i):
        src = (sp_lo, sp_hi, sq, sq)[i].at[k, c]
        dst = (rp_hi, rp_lo, rq_r, rq_l)[i].at[k, c]
        return remote(src, dst, halo_s.at[k, c, i], halo_r.at[k, c, i], peer[i])

    def vel_copy(c, i):
        src = (ss_lo, ss_hi, sdq, sdq)[i].at[c]
        dst = (rs_hi, rs_lo, rd_r, rd_l)[i].at[c]
        return remote(src, dst, vel_s.at[c, i], vel_r.at[c, i], peer[i])

    def buo_copy(i):
        src = (bx.at[pl.ds(OFF, 8), :], bx.at[pl.ds(END - 8, 8), :], bq, bq)[i]
        dst = (rb_hi, rb_lo, rbq_r, rbq_l)[i]
        return remote(src, dst, buo_s.at[i], buo_r.at[i], peer[i])

    def each_side(make, what):
        for i in range(4):
            cond = has[i ^ 1] if what == "recv" else has[i]

            @pl.when(cond)
            def _(i=i):
                copy = make(i)
                if what == "start":
                    copy.start()
                elif what == "recv":
                    copy.wait_recv()
                else:
                    copy.wait_send()

    def sens_copy(o):
        return remote(sens, sens_all.at[di], sens_s.at[o - 1], sens_r.at[o - 1], dip_peer(o))

    each_side(buo_copy, "start")
    for o in range(1, nd):
        sens_copy(o).start()

    zero_pack = jnp.zeros((rows, 128), jnp.float32)

    def packed(acc, field, j):
        return jnp.where(slot == j, pltpu.roll(field, 8 * j + 4, 1), acc)

    in_p.wait()
    in_s.wait()
    in_d.wait()

    for c in reversed(range(nch)):

        def pack_first(j, accs, c=c):
            lev = c * CH + j
            f = pe[lev + 1, pl.ds(OFF, rows), :]
            sp_lo[0, c, j] = f[0:4]
            sp_hi[0, c, j] = f[rows - 4 : rows]
            ss_lo[c, j] = se[lev, pl.ds(OFF, 8), :][0:2]
            ss_hi[c, j] = se[lev, pl.ds(END - 8, 8), :][6:8]
            return packed(accs[0], f, j), packed(accs[1], dv[lev], j)

        a, b = lax.fori_loop(0, CH, pack_first, (zero_pack, zero_pack), unroll=8)
        sq[0, c] = a
        sdq[c] = b
        each_side(lambda i, c=c: halo_copy(0, c, i), "start")
        each_side(lambda i, c=c: vel_copy(c, i), "start")

    in_k.wait()

    def widen(i, _):
        kf[pl.ds(pl.multiple_of(i * rows, rows), rows), :] = kv[i].astype(jnp.float32)
        return 0

    lax.fori_loop(0, probes, widen, 0, unroll=8)
    half = rows // 2

    def regroup(x, _):
        kt[x, :, 0:128] = kf[pl.ds(x, probes, stride=rows), :].astype(jnp.bfloat16)
        kt[x, :, 128:256] = kf[pl.ds(x + half, probes, stride=rows), :].astype(jnp.bfloat16)
        return 0

    lax.fori_loop(0, half, regroup, 0, unroll=4)

    sens_all[di] = sens[...]
    for o in range(1, nd):
        sens_copy(o).wait_recv()
    every = sens_all[...].reshape(nd * 8, 128)
    mine = every[:, 5:6] == di.astype(jnp.float32)
    cell = every[:, 4:5].astype(jnp.int32)
    slane = lax.broadcasted_iota(jnp.int32, (nd * 8, 128), 1)
    at_row = (lax.shift_right_logical(cell, 7) == slane) & mine
    at_col = ((cell & 127) == slane).astype(jnp.float32)
    for k in range(STEPS):
        left = jnp.where(at_row, every[:, k : k + 1], 0.0)
        placed = lax.dot_general(
            left,
            at_col,
            (((0,), (0,)), ((), ())),
            precision=lax.Precision.HIGHEST,
            preferred_element_type=jnp.float32,
        )
        inj[k] = placed[0:rows]

    each_side(buo_copy, "recv")
    bx[pl.ds(OFF - 8, 8), :] = rb_lo[...]
    bx[pl.ds(END, 8), :] = rb_hi[...]
    hb[...] = jnp.where(low, rbq_l[...], rbq_r[...])

    def phase_a(k, c):
        each_side(lambda i: halo_copy(k, c, i), "recv")
        base = c * CH

        @pl.when(k == 0)
        def _():
            each_side(lambda i: vel_copy(c, i), "recv")
            hv[c] = jnp.where(low, rd_l[c], rd_r[c])
            se[pl.ds(base, CH), pl.ds(OFF - 2, 2), :] = rs_lo[c]
            se[pl.ds(base, CH), pl.ds(END, 2), :] = rs_hi[c]

        pe[pl.ds(base + 1, CH), pl.ds(OFF - 4, 4), :] = rp_lo[k, c]
        pe[pl.ds(base + 1, CH), pl.ds(END, 4), :] = rp_hi[k, c]
        own = sq[k, c]
        d_left = lane_diff(jnp.where(low, rq_l[k, c], own))
        d_right = lane_diff(jnp.where(low, own, rq_r[k, c]))
        hv[c] = hv[c] - hb[...] * jnp.where(low, d_left, d_right)
        edge_a[...] = jnp.where(low, d_right, d_left)

        def level(j, acc):
            lev = base + j

            def win(o):
                return pe[lev + 1, pl.ds(OFF - 8 + o, rows + 16), :]

            ds = 8.0 * (win(1) - win(-1)) - (win(2) - win(-2))
            ext = pl.ds(OFF - 8, rows + 16)
            se[lev, ext, :] = se[lev, ext, :] - bx[ext, :] * ds
            own_rows = pl.ds(OFF, rows)
            b = bx[own_rows, :]
            dd = jnp.where(rim, pltpu.roll(edge_a[...], 124 - 8 * j, 1), lane_diff(pe[lev + 1, own_rows, :]))
            v = dv[lev] - b * dd
            dv[lev] = v
            dz = (6.0 * b) * (pe[lev + 2, own_rows, :] - pe[lev, own_rows, :])
            vv[lev + 1] = vv[lev + 1] - dz
            return packed(acc, v, j)

        acc = zero_pack
        for j in range(CH):
            acc = level(j, acc)
        qv[c] = acc

    def phase_b(k, c):
        base = c * CH
        own = qv[c]
        halo = hv[c]
        d_left = lane_diff(jnp.where(low, halo, own))
        d_right = lane_diff(jnp.where(low, own, halo))
        edge_b[...] = jnp.where(low, d_right, d_left)

        def level(j, acc):
            lev = base + j

            def win(o):
                return se[lev, pl.ds(OFF + o, rows), :]

            ds = 8.0 * (win(1) - win(-1)) - (win(2) - win(-2))
            dd = jnp.where(rim, pltpu.roll(edge_b[...], 124 - 8 * j, 1), lane_diff(dv[lev]))
            dz = 6.0 * (vv[lev + 2] - vv[lev])
            own_rows = pl.ds(OFF, rows)
            f = pe[lev + 1, own_rows, :] - bk[...] * (ds + dd + dz) + (TIME_STEP * grav[lev]) * vv[lev + 1]
            if j == CH - 1:
                f = f + jnp.where(c == nch - 1, inj[k], 0.0)
            pe[lev + 1, own_rows, :] = f
            sp_lo[k + 1, c, j] = f[0:4]
            sp_hi[k + 1, c, j] = f[rows - 4 : rows]
            return packed(acc, f, j)

        acc = zero_pack
        for j in range(CH):
            acc = level(j, acc)
        sq[k + 1, c] = acc

        @pl.when(k < STEPS - 1)
        def _():
            each_side(lambda i: halo_copy(k + 1, c, i), "start")

        @pl.when(k == STEPS - 1)
        def _():
            out_copy(c).start()

    def out_copy(c):
        return pltpu.make_async_copy(
            pe.at[pl.ds(1 + c * CH, CH), pl.ds(OFF, rows), :], out_p.at[pl.ds(c * CH, CH)], out_sem.at[c]
        )

    share = gram.shape[1]

    def red1(o):
        to = lax.rem(di + o, nd)
        return remote(gram.at[to], part1.at[o - 1], red1_s.at[o - 1], red1_r.at[o - 1], dip_peer(o))

    def red2(o):
        return remote(part2.at[si], part2.at[si], red2_s.at[o - 1], red2_r.at[o - 1], strike_peer(o))

    def red3(o):
        return remote(out_g.at[di], out_g.at[di], red3_s.at[o - 1], red3_r.at[o - 1], dip_peer(o))

    def reduce_start():
        sea = pe[levels, pl.ds(OFF, rows), :] * scale
        wrow[...] = sea * sea

        def body(x, acc):
            kx = kt[x]
            w = jnp.concatenate([wrow[pl.ds(x, 1), :], wrow[pl.ds(x + half, 1), :]], axis=1)
            kw = kx.astype(jnp.float32) * w
            hi = kw.astype(jnp.bfloat16)
            lo = (kw - hi.astype(jnp.float32)).astype(jnp.bfloat16)
            both = jnp.concatenate([hi, lo], axis=0)
            return acc + lax.dot_general(
                both, kx, (((1,), (1,)), ((), ())), preferred_element_type=jnp.float32
            )

        acc = lax.fori_loop(0, half, body, jnp.zeros((2 * probes, probes), jnp.float32), unroll=8)
        total = acc[0:probes] + acc[probes : 2 * probes]
        total = jnp.concatenate([total, jnp.zeros((probes, 128 - probes), jnp.float32)], axis=1)
        if nd * share > probes:
            total = jnp.concatenate([total, jnp.zeros((nd * share - probes, 128), jnp.float32)], axis=0)
        for d in range(nd):
            gram[d] = total[d * share : (d + 1) * share]
        for o in range(1, nd):
            red1(o).start()

    def reduce_middle():
        s = gram[di]
        for o in range(1, nd):
            red1(o).wait_recv()
            s = s + part1[o - 1]
        part2[si] = s
        for o in range(1, ns):
            red2(o).start()

    def reduce_spread():
        for o in range(1, ns):
            red2(o).wait_recv()
        s = part2[0]
        for i in range(1, ns):
            s = s + part2[i]
        out_g[di] = s
        for o in range(1, nd):
            red3(o).start()

    def turn(t, _):
        k = t // (nch + 1)
        i = t % (nch + 1)

        @pl.when(i < nch)
        def _():
            phase_a(k, nch - 1 - i)

        @pl.when(i > 0)
        def _():
            phase_b(k, nch - i)

        for at, stage in ((1, reduce_start), (2, reduce_middle), (3, reduce_spread)):

            @pl.when((k == STEPS - 1) & (i == at))
            def _(stage=stage):
                stage()

        return 0

    lax.fori_loop(0, STEPS * (nch + 1), turn, 0)

    for c in range(nch):
        out_copy(c).wait()
        each_side(lambda i, c=c: vel_copy(c, i), "send")
        for k in range(STEPS):
            each_side(lambda i, c=c, k=k: halo_copy(k, c, i), "send")
    each_side(buo_copy, "send")
    for o in range(1, nd):
        sens_copy(o).wait_send()
        red1(o).wait_send()
        red3(o).wait_recv()
        red3(o).wait_send()
    for o in range(1, ns):
        red2(o).wait_send()


def body(
    ns,
    nd,
    pressure,
    strike_vel,
    dip_vel,
    bathy_class,
    bulk_table,
    buoy_table,
    gravity,
    sensor_amp,
    sensor_owner,
    sensor_cell,
    probe_kernel,
):
    levels, rows, cols = pressure.shape
    probes = probe_kernel.shape[0]
    nch = levels // CH
    share = -(-probes // (8 * nd)) * 8
    scale = 1.0 / math.sqrt(rows * cols * ns * nd)
    sens = jnp.concatenate(
        [
            sensor_amp.T,
            sensor_cell.astype(jnp.float32)[:, None],
            sensor_owner.astype(jnp.float32),
            jnp.zeros((sensor_amp.shape[1], 128 - STEPS - 2), jnp.float32),
        ],
        axis=1,
    )
    f32 = jnp.float32

    def vmem(*shape, dtype=f32):
        return pltpu.VMEM(shape, dtype)

    def sems(*shape):
        return pltpu.SemaphoreType.DMA(shape)

    scratch = [
        vmem(levels + 2, rows + 2 * OFF, cols),
        vmem(levels, rows + 2 * OFF, cols),
        vmem(levels, rows, cols),
        vmem(levels + 2, rows, cols),
        vmem(probes, rows, cols, dtype=jnp.bfloat16),
        vmem(probes * rows, cols),
        vmem(rows // 2, probes, 2 * cols, dtype=jnp.bfloat16),
        vmem(rows + 2 * OFF, cols),
        vmem(rows, cols),
        vmem(rows, cols),
        vmem(rows, cols),
        vmem(STEPS, rows, cols),
        vmem(rows, cols),
        vmem(STEPS + 1, nch, CH, 4, cols),
        vmem(STEPS + 1, nch, CH, 4, cols),
        vmem(STEPS, nch, CH, 4, cols),
        vmem(STEPS, nch, CH, 4, cols),
        vmem(STEPS + 1, nch, rows, cols),
        vmem(STEPS, nch, rows, cols),
        vmem(STEPS, nch, rows, cols),
        vmem(nch, CH, 2, cols),
        vmem(nch, CH, 2, cols),
        vmem(nch, CH, 2, cols),
        vmem(nch, CH, 2, cols),
        vmem(nch, rows, cols),
        vmem(nch, rows, cols),
        vmem(nch, rows, cols),
        vmem(8, cols),
        vmem(8, cols),
        vmem(rows, cols),
        vmem(rows, cols),
        vmem(nch, rows, cols),
        vmem(nch, rows, cols),
        vmem(rows, cols),
        vmem(rows, cols),
        vmem(nd, 8, cols),
        vmem(nd, share, cols),
        vmem(nd - 1, share, cols),
        vmem(ns, share, cols),
        sems(4),
        sems(nch),
        sems(STEPS, nch, 4),
        sems(STEPS, nch, 4),
        sems(nch, 4),
        sems(nch, 4),
        sems(4),
        sems(4),
        sems(nd - 1),
        sems(nd - 1),
        sems(nd - 1),
        sems(nd - 1),
        sems(ns - 1),
        sems(ns - 1),
        sems(nd - 1),
        sems(nd - 1),
    ]
    smem = pl.BlockSpec(memory_space=pltpu.SMEM)
    whole = pl.BlockSpec(memory_space=pltpu.VMEM)
    hbm = pl.BlockSpec(memory_space=pl.ANY)
    final, gram = pl.pallas_call(
        functools.partial(kernel, ns, nd, scale),
        out_shape=(
            jax.ShapeDtypeStruct(pressure.shape, f32),
            jax.ShapeDtypeStruct((nd, share, cols), f32),
        ),
        in_specs=[smem, smem, smem, whole, whole, hbm, hbm, hbm, hbm],
        out_specs=(hbm, whole),
        scratch_shapes=scratch,
        compiler_params=pltpu.CompilerParams(
            collective_id=0, has_side_effects=True, vmem_limit_bytes=60 * 2**20
        ),
    )(bulk_table, buoy_table, gravity, bathy_class, sens, pressure, strike_vel, dip_vel, probe_kernel)
    gram = gram.reshape(nd * share, cols)[:probes, :probes]
    return final, jnp.linalg.cholesky(gram).T


def solution(mesh):
    return jax.shard_map(
        functools.partial(body, mesh.shape["strike"], mesh.shape["dip"]),
        mesh=mesh,
        in_specs=(
            P(None, "strike", "dip"),
            P(None, "strike", "dip"),
            P(None, "strike", "dip"),
            P("strike", "dip"),
            P(),
            P(),
            P(),
            P(None, ("strike", "dip")),
            P(("strike", "dip"), None),
            P(("strike", "dip")),
            P(None, "strike", "dip"),
        ),
        out_specs=(P(None, "strike", "dip"), P()),
        check_vma=False,
    )
```

```python
import functools
import math

import jax
import jax.numpy as jnp
from jax import lax
from jax.experimental import pallas as pl
from jax.experimental.pallas import tpu as pltpu
from jax.sharding import PartitionSpec as P

MESH = pl.DeviceIdType.MESH
STEPS = 4
NCLASS = 8
TIME_STEP = 0.2
OFF = 16
CH = 16


def lane_diff(f):
    n = f.shape[-1]
    ax = f.ndim - 1
    near = pltpu.roll(f, n - 1, ax) - pltpu.roll(f, 1, ax)
    far = pltpu.roll(f, n - 2, ax) - pltpu.roll(f, 2, ax)
    return 8.0 * near - far


def kernel(
    ns,
    nd,
    scale,
    bulk_t,
    buoy_t,
    grav,
    classes,
    sens,
    p_hbm,
    sv_hbm,
    dv_hbm,
    k_hbm,
    out_p,
    out_g,
    pe,
    se,
    dv,
    vv,
    kv,
    kf,
    kt,
    bx,
    bk,
    bq,
    hb,
    inj,
    wrow,
    sp_lo,
    sp_hi,
    rp_lo,
    rp_hi,
    sq,
    rq_l,
    rq_r,
    ss_lo,
    ss_hi,
    rs_lo,
    rs_hi,
    sdq,
    rd_l,
    rd_r,
    rb_lo,
    rb_hi,
    rbq_l,
    rbq_r,
    hv,
    qv,
    edge_a,
    edge_b,
    inner_a,
    inner_b,
    dmat,
    sens_all,
    gram,
    part1,
    part2,
    in_sem,
    out_sem,
    halo_s,
    halo_r,
    vel_s,
    vel_r,
    buo_s,
    buo_r,
    sens_s,
    sens_r,
    red1_s,
    red1_r,
    red2_s,
    red2_r,
    red3_s,
    red3_r,
):
    levels = p_hbm.shape[0]
    rows = p_hbm.shape[1]
    nch = levels // CH
    probes = k_hbm.shape[0]
    si = lax.axis_index("strike")
    di = lax.axis_index("dip")
    END = OFF + rows

    def strike_peer(o):
        return (lax.rem(si + o, ns), di)

    def dip_peer(o):
        return (si, lax.rem(di + o, nd))

    has = (si > 0, si < ns - 1, di > 0, di < nd - 1)
    peer = ((si - 1, di), (si + 1, di), (si, di - 1), (si, di + 1))

    in_p = pltpu.make_async_copy(p_hbm, pe.at[pl.ds(1, levels), pl.ds(OFF, rows), :], in_sem.at[0])
    in_s = pltpu.make_async_copy(sv_hbm, se.at[:, pl.ds(OFF, rows), :], in_sem.at[1])
    in_d = pltpu.make_async_copy(dv_hbm, dv, in_sem.at[2])
    in_k = pltpu.make_async_copy(k_hbm, kv, in_sem.at[3])
    in_p.start()
    in_s.start()
    in_d.start()
    in_k.start()

    barrier = pltpu.get_barrier_semaphore()
    for o in range(1, ns):
        pl.semaphore_signal(barrier, inc=1, device_id=strike_peer(o), device_id_type=MESH)
    for o in range(1, nd):
        pl.semaphore_signal(barrier, inc=1, device_id=dip_peer(o), device_id_type=MESH)

    lane = lax.broadcasted_iota(jnp.int32, (rows, 128), 1)
    slot = lane // 8
    low = (lane % 8) < 4
    rim = (lane < 2) | (lane >= 126)

    cls = classes[...]
    buoy = jnp.zeros((rows, 128), jnp.float32)
    bulk = jnp.zeros((rows, 128), jnp.float32)
    for i in range(NCLASS):
        buoy = jnp.where(cls == i, buoy_t[i], buoy)
        bulk = jnp.where(cls == i, bulk_t[i], bulk)
    bk[...] = bulk * (TIME_STEP / 12.0)
    bx[pl.ds(OFF, rows), :] = buoy * (TIME_STEP / 12.0)
    first = jnp.where(lane < 8, pltpu.roll(buoy * (TIME_STEP / 12.0), 4, 1), 0.0)
    for width in (8, 16, 32, 64):
        first = first + pltpu.roll(first, width, 1)
    bq[...] = first

    zero_block = jnp.zeros((rows, 128), jnp.float32)
    pe[0, pl.ds(OFF, rows), :] = zero_block
    pe[levels + 1, pl.ds(OFF, rows), :] = zero_block

    def clear(i, _):
        vv[i] = zero_block
        return 0

    lax.fori_loop(0, levels + 2, clear, 0)

    def zero_when(cond, *refs):
        @pl.when(jnp.logical_not(cond))
        def _():
            for r in refs:
                r[...] = jnp.zeros(r.shape, r.dtype)

    zero_when(has[0], rp_lo, rs_lo, rb_lo)
    zero_when(has[1], rp_hi, rs_hi, rb_hi)
    zero_when(has[2], rq_l, rd_l, rbq_l)
    zero_when(has[3], rq_r, rd_r, rbq_r)

    pl.semaphore_wait(barrier, ns - 1 + nd - 1)

    def remote(src, dst, s, r, to):
        return pltpu.make_async_remote_copy(
            src_ref=src, dst_ref=dst, send_sem=s, recv_sem=r, device_id=to, device_id_type=MESH
        )

    def halo_copy(k, c, i):
        src = (sp_lo, sp_hi, sq, sq)[i].at[k, c]
        dst = (rp_hi, rp_lo, rq_r, rq_l)[i].at[k, c]
        return remote(src, dst, halo_s.at[k, c, i], halo_r.at[k, c, i], peer[i])

    def vel_copy(c, i):
        src = (ss_lo, ss_hi, sdq, sdq)[i].at[c]
        dst = (rs_hi, rs_lo, rd_r, rd_l)[i].at[c]
        return remote(src, dst, vel_s.at[c, i], vel_r.at[c, i], peer[i])

    def buo_copy(i):
        src = (bx.at[pl.ds(OFF, 8), :], bx.at[pl.ds(END - 8, 8), :], bq, bq)[i]
        dst = (rb_hi, rb_lo, rbq_r, rbq_l)[i]
        return remote(src, dst, buo_s.at[i], buo_r.at[i], peer[i])

    def each_side(make, what):
        for i in range(4):
            cond = has[i ^ 1] if what == "recv" else has[i]

            @pl.when(cond)
            def _(i=i):
                copy = make(i)
                if what == "start":
                    copy.start()
                elif what == "recv":
                    copy.wait_recv()
                else:
                    copy.wait_send()

    def sens_copy(o):
        return remote(sens, sens_all.at[di], sens_s.at[o - 1], sens_r.at[o - 1], dip_peer(o))

    each_side(buo_copy, "start")
    for o in range(1, nd):
        sens_copy(o).start()

    zero_pack = jnp.zeros((rows, 128), jnp.float32)

    def packed(acc, field, j):
        return jnp.where(slot == j, pltpu.roll(field, 8 * j + 4, 1), acc)

    in_p.wait()
    in_s.wait()
    in_d.wait()

    for c in reversed(range(nch)):

        def pack_first(j, accs, c=c):
            lev = c * CH + j
            f = pe[lev + 1, pl.ds(OFF, rows), :]
            sp_lo[0, c, j] = f[0:4]
            sp_hi[0, c, j] = f[rows - 4 : rows]
            ss_lo[c, j] = se[lev, pl.ds(OFF, 8), :][0:2]
            ss_hi[c, j] = se[lev, pl.ds(END - 8, 8), :][6:8]
            return packed(accs[0], f, j), packed(accs[1], dv[lev], j)

        a, b = lax.fori_loop(0, CH, pack_first, (zero_pack, zero_pack), unroll=8)
        sq[0, c] = a
        sdq[c] = b
        each_side(lambda i, c=c: halo_copy(0, c, i), "start")
        each_side(lambda i, c=c: vel_copy(c, i), "start")

    in_k.wait()

    def widen(i, _):
        kf[pl.ds(pl.multiple_of(i * rows, rows), rows), :] = kv[i].astype(jnp.float32)
        return 0

    lax.fori_loop(0, probes, widen, 0, unroll=8)
    half = rows // 2

    def regroup(x, _):
        kt[x, :, 0:128] = kf[pl.ds(x, probes, stride=rows), :].astype(jnp.bfloat16)
        kt[x, :, 128:256] = kf[pl.ds(x + half, probes, stride=rows), :].astype(jnp.bfloat16)
        return 0

    lax.fori_loop(0, half, regroup, 0, unroll=4)

    sens_all[di] = sens[...]
    for o in range(1, nd):
        sens_copy(o).wait_recv()
    every = sens_all[...].reshape(nd * 8, 128)
    mine = every[:, 5:6] == di.astype(jnp.float32)
    cell = every[:, 4:5].astype(jnp.int32)
    slane = lax.broadcasted_iota(jnp.int32, (nd * 8, 128), 1)
    at_row = (lax.shift_right_logical(cell, 7) == slane) & mine
    at_col = ((cell & 127) == slane).astype(jnp.float32)
    for k in range(STEPS):
        left = jnp.where(at_row, every[:, k : k + 1], 0.0)
        placed = lax.dot_general(
            left,
            at_col,
            (((0,), (0,)), ((), ())),
            precision=lax.Precision.HIGHEST,
            preferred_element_type=jnp.float32,
        )
        inj[k] = placed[0:rows]

    each_side(buo_copy, "recv")
    bx[pl.ds(OFF - 8, 8), :] = rb_lo[...]
    bx[pl.ds(END, 8), :] = rb_hi[...]
    hb[...] = jnp.where(low, rbq_l[...], rbq_r[...])

    gap = lax.broadcasted_iota(jnp.int32, (256, 128), 0) - lax.broadcasted_iota(jnp.int32, (256, 128), 1)
    gap = (gap + 256) & 127
    weights = jnp.where(gap == 1, 8.0, 0.0) - jnp.where(gap == 127, 8.0, 0.0)
    weights = weights - jnp.where(gap == 2, 1.0, 0.0) + jnp.where(gap == 126, 1.0, 0.0)
    dmat[...] = weights.astype(jnp.bfloat16)

    def product_diff(f):
        flat = f.reshape(4 * rows, 128)
        hi = flat.astype(jnp.bfloat16)
        lo = (flat - hi.astype(jnp.float32)).astype(jnp.bfloat16)
        both = jnp.concatenate([hi, lo], axis=1)
        return jnp.dot(both, dmat[...], preferred_element_type=jnp.float32).reshape(4, rows, 128)

    def phase_a(k, c):
        each_side(lambda i: halo_copy(k, c, i), "recv")
        base = c * CH

        @pl.when(k == 0)
        def _():
            each_side(lambda i: vel_copy(c, i), "recv")
            hv[c] = jnp.where(low, rd_l[c], rd_r[c])
            se[pl.ds(base, CH), pl.ds(OFF - 2, 2), :] = rs_lo[c]
            se[pl.ds(base, CH), pl.ds(END, 2), :] = rs_hi[c]

        pe[pl.ds(base + 1, CH), pl.ds(OFF - 4, 4), :] = rp_lo[k, c]
        pe[pl.ds(base + 1, CH), pl.ds(END, 4), :] = rp_hi[k, c]
        own = sq[k, c]
        d_left = lane_diff(jnp.where(low, rq_l[k, c], own))
        d_right = lane_diff(jnp.where(low, own, rq_r[k, c]))
        hv[c] = hv[c] - hb[...] * jnp.where(low, d_left, d_right)
        edge_a[...] = jnp.where(low, d_right, d_left)
        for g in range(0, CH, 4):
            inner_a[g : g + 4] = product_diff(pe[pl.ds(base + 1 + g, 4), pl.ds(OFF, rows), :])

        def level(j, acc):
            lev = base + j

            def win(o):
                return pe[lev + 1, pl.ds(OFF - 8 + o, rows + 16), :]

            ds = 8.0 * (win(1) - win(-1)) - (win(2) - win(-2))
            ext = pl.ds(OFF - 8, rows + 16)
            se[lev, ext, :] = se[lev, ext, :] - bx[ext, :] * ds
            own_rows = pl.ds(OFF, rows)
            b = bx[own_rows, :]
            dd = jnp.where(rim, pltpu.roll(edge_a[...], 124 - 8 * j, 1), inner_a[j])
            v = dv[lev] - b * dd
            dv[lev] = v
            dz = (6.0 * b) * (pe[lev + 2, own_rows, :] - pe[lev, own_rows, :])
            vv[lev + 1] = vv[lev + 1] - dz
            return packed(acc, v, j)

        acc = zero_pack
        for j in range(CH):
            acc = level(j, acc)
        qv[c] = acc

    def phase_b(k, c):
        base = c * CH
        own = qv[c]
        halo = hv[c]
        d_left = lane_diff(jnp.where(low, halo, own))
        d_right = lane_diff(jnp.where(low, own, halo))
        edge_b[...] = jnp.where(low, d_right, d_left)
        for g in range(0, CH, 4):
            inner_b[g : g + 4] = product_diff(dv[pl.ds(base + g, 4)])

        def level(j, acc):
            lev = base + j

            def win(o):
                return se[lev, pl.ds(OFF + o, rows), :]

            ds = 8.0 * (win(1) - win(-1)) - (win(2) - win(-2))
            dd = jnp.where(rim, pltpu.roll(edge_b[...], 124 - 8 * j, 1), inner_b[j])
            dz = 6.0 * (vv[lev + 2] - vv[lev])
            own_rows = pl.ds(OFF, rows)
            f = pe[lev + 1, own_rows, :] - bk[...] * (ds + dd + dz) + (TIME_STEP * grav[lev]) * vv[lev + 1]
            if j == CH - 1:
                f = f + jnp.where(c == nch - 1, inj[k], 0.0)
            pe[lev + 1, own_rows, :] = f
            sp_lo[k + 1, c, j] = f[0:4]
            sp_hi[k + 1, c, j] = f[rows - 4 : rows]
            return packed(acc, f, j)

        acc = zero_pack
        for j in range(CH):
            acc = level(j, acc)
        sq[k + 1, c] = acc

        @pl.when(k < STEPS - 1)
        def _():
            each_side(lambda i: halo_copy(k + 1, c, i), "start")

        @pl.when(k == STEPS - 1)
        def _():
            out_copy(c).start()

    def out_copy(c):
        return pltpu.make_async_copy(
            pe.at[pl.ds(1 + c * CH, CH), pl.ds(OFF, rows), :], out_p.at[pl.ds(c * CH, CH)], out_sem.at[c]
        )

    share = gram.shape[1]

    def red1(o):
        to = lax.rem(di + o, nd)
        return remote(gram.at[to], part1.at[o - 1], red1_s.at[o - 1], red1_r.at[o - 1], dip_peer(o))

    def red2(o):
        return remote(part2.at[si], part2.at[si], red2_s.at[o - 1], red2_r.at[o - 1], strike_peer(o))

    def red3(o):
        return remote(out_g.at[di], out_g.at[di], red3_s.at[o - 1], red3_r.at[o - 1], dip_peer(o))

    def reduce_start():
        sea = pe[levels, pl.ds(OFF, rows), :] * scale
        wrow[...] = sea * sea

        def body(x, acc):
            kx = kt[x]
            w = jnp.concatenate([wrow[pl.ds(x, 1), :], wrow[pl.ds(x + half, 1), :]], axis=1)
            kw = kx.astype(jnp.float32) * w
            hi = kw.astype(jnp.bfloat16)
            lo = (kw - hi.astype(jnp.float32)).astype(jnp.bfloat16)
            both = jnp.concatenate([hi, lo], axis=0)
            return acc + lax.dot_general(
                both, kx, (((1,), (1,)), ((), ())), preferred_element_type=jnp.float32
            )

        acc = lax.fori_loop(0, half, body, jnp.zeros((2 * probes, probes), jnp.float32), unroll=8)
        total = acc[0:probes] + acc[probes : 2 * probes]
        total = jnp.concatenate([total, jnp.zeros((probes, 128 - probes), jnp.float32)], axis=1)
        if nd * share > probes:
            total = jnp.concatenate([total, jnp.zeros((nd * share - probes, 128), jnp.float32)], axis=0)
        for d in range(nd):
            gram[d] = total[d * share : (d + 1) * share]
        for o in range(1, nd):
            red1(o).start()

    def reduce_middle():
        s = gram[di]
        for o in range(1, nd):
            red1(o).wait_recv()
            s = s + part1[o - 1]
        part2[si] = s
        for o in range(1, ns):
            red2(o).start()

    def reduce_spread():
        for o in range(1, ns):
            red2(o).wait_recv()
        s = part2[0]
        for i in range(1, ns):
            s = s + part2[i]
        out_g[di] = s
        for o in range(1, nd):
            red3(o).start()

    def turn(t, _):
        k = t // (nch + 1)
        i = t % (nch + 1)

        @pl.when(i < nch)
        def _():
            phase_a(k, nch - 1 - i)

        @pl.when(i > 0)
        def _():
            phase_b(k, nch - i)

        for at, stage in ((1, reduce_start), (2, reduce_middle), (3, reduce_spread)):

            @pl.when((k == STEPS - 1) & (i == at))
            def _(stage=stage):
                stage()

        return 0

    lax.fori_loop(0, STEPS * (nch + 1), turn, 0)

    for c in range(nch):
        out_copy(c).wait()
        each_side(lambda i, c=c: vel_copy(c, i), "send")
        for k in range(STEPS):
            each_side(lambda i, c=c, k=k: halo_copy(k, c, i), "send")
    each_side(buo_copy, "send")
    for o in range(1, nd):
        sens_copy(o).wait_send()
        red1(o).wait_send()
        red3(o).wait_recv()
        red3(o).wait_send()
    for o in range(1, ns):
        red2(o).wait_send()


def body(
    ns,
    nd,
    pressure,
    strike_vel,
    dip_vel,
    bathy_class,
    bulk_table,
    buoy_table,
    gravity,
    sensor_amp,
    sensor_owner,
    sensor_cell,
    probe_kernel,
):
    levels, rows, cols = pressure.shape
    probes = probe_kernel.shape[0]
    nch = levels // CH
    share = -(-probes // (8 * nd)) * 8
    scale = 1.0 / math.sqrt(rows * cols * ns * nd)
    sens = jnp.concatenate(
        [
            sensor_amp.T,
            sensor_cell.astype(jnp.float32)[:, None],
            sensor_owner.astype(jnp.float32),
            jnp.zeros((sensor_amp.shape[1], 128 - STEPS - 2), jnp.float32),
        ],
        axis=1,
    )
    f32 = jnp.float32

    def vmem(*shape, dtype=f32):
        return pltpu.VMEM(shape, dtype)

    def sems(*shape):
        return pltpu.SemaphoreType.DMA(shape)

    scratch = [
        vmem(levels + 2, rows + 2 * OFF, cols),
        vmem(levels, rows + 2 * OFF, cols),
        vmem(levels, rows, cols),
        vmem(levels + 2, rows, cols),
        vmem(probes, rows, cols, dtype=jnp.bfloat16),
        vmem(probes * rows, cols),
        vmem(rows // 2, probes, 2 * cols, dtype=jnp.bfloat16),
        vmem(rows + 2 * OFF, cols),
        vmem(rows, cols),
        vmem(rows, cols),
        vmem(rows, cols),
        vmem(STEPS, rows, cols),
        vmem(rows, cols),
        vmem(STEPS + 1, nch, CH, 4, cols),
        vmem(STEPS + 1, nch, CH, 4, cols),
        vmem(STEPS, nch, CH, 4, cols),
        vmem(STEPS, nch, CH, 4, cols),
        vmem(STEPS + 1, nch, rows, cols),
        vmem(STEPS, nch, rows, cols),
        vmem(STEPS, nch, rows, cols),
        vmem(nch, CH, 2, cols),
        vmem(nch, CH, 2, cols),
        vmem(nch, CH, 2, cols),
        vmem(nch, CH, 2, cols),
        vmem(nch, rows, cols),
        vmem(nch, rows, cols),
        vmem(nch, rows, cols),
        vmem(8, cols),
        vmem(8, cols),
        vmem(rows, cols),
        vmem(rows, cols),
        vmem(nch, rows, cols),
        vmem(nch, rows, cols),
        vmem(rows, cols),
        vmem(rows, cols),
        vmem(CH, rows, cols),
        vmem(CH, rows, cols),
        vmem(2 * cols, cols, dtype=jnp.bfloat16),
        vmem(nd, 8, cols),
        vmem(nd, share, cols),
        vmem(nd - 1, share, cols),
        vmem(ns, share, cols),
        sems(4),
        sems(nch),
        sems(STEPS, nch, 4),
        sems(STEPS, nch, 4),
        sems(nch, 4),
        sems(nch, 4),
        sems(4),
        sems(4),
        sems(nd - 1),
        sems(nd - 1),
        sems(nd - 1),
        sems(nd - 1),
        sems(ns - 1),
        sems(ns - 1),
        sems(nd - 1),
        sems(nd - 1),
    ]
    smem = pl.BlockSpec(memory_space=pltpu.SMEM)
    whole = pl.BlockSpec(memory_space=pltpu.VMEM)
    hbm = pl.BlockSpec(memory_space=pl.ANY)
    final, gram = pl.pallas_call(
        functools.partial(kernel, ns, nd, scale),
        out_shape=(
            jax.ShapeDtypeStruct(pressure.shape, f32),
            jax.ShapeDtypeStruct((nd, share, cols), f32),
        ),
        in_specs=[smem, smem, smem, whole, whole, hbm, hbm, hbm, hbm],
        out_specs=(hbm, whole),
        scratch_shapes=scratch,
        compiler_params=pltpu.CompilerParams(
            collective_id=0, has_side_effects=True, vmem_limit_bytes=60 * 2**20
        ),
    )(bulk_table, buoy_table, gravity, bathy_class, sens, pressure, strike_vel, dip_vel, probe_kernel)
    gram = gram.reshape(nd * share, cols)[:probes, :probes]
    return final, jnp.linalg.cholesky(gram).T


def solution(mesh):
    return jax.shard_map(
        functools.partial(body, mesh.shape["strike"], mesh.shape["dip"]),
        mesh=mesh,
        in_specs=(
            P(None, "strike", "dip"),
            P(None, "strike", "dip"),
            P(None, "strike", "dip"),
            P("strike", "dip"),
            P(),
            P(),
            P(),
            P(None, ("strike", "dip")),
            P(("strike", "dip"), None),
            P(("strike", "dip")),
            P(None, "strike", "dip"),
        ),
        out_specs=(P(None, "strike", "dip"), P()),
        check_vma=False,
    )
```
